32 devices in a mesh: pairs: 8 (over z, core), cols: 4 (over y, x).
Axes of the slice: x: 2, y: 2, z: 4, core: 2. Of those that a mesh axis runs over, the one named last changes fastest.
Arguments:
- pair_list: int32 [48, 5], P('pairs'), may hold values from 0 to 7, as said below
- near_tile_block: bfloat16 [48, 2048, 2048], P('pairs', None, 'cols'), may hold values from -0.0546875 to 0.0546875
- history: float32 [4, 16, 32, 2048], P(None, 'pairs', None, 'cols'), may hold values from -6 to 6
- excitation: float32 [4, 16, 32, 2048], P(None, 'pairs', None, 'cols'), may hold values from -6 to 6
- diagonal: float32 [16, 2048], P('pairs', 'cols'), may hold values from 2 to 4
Outputs:
- densities: float32 [4, 16, 32, 2048], P(None, 'pairs', None, 'cols')
The draws below stay inside these ranges and needn't reach their ends.
Inputs may be any that keep to these rules, and one draw needn't show every extreme that they name: `pair_list`: rows s * 6 to s * 6 + 5 are the slots of index s of pairs. Column 0 and column 2 are below 2, column 1 below 8, column 3 below 4, column 4 is 0 or 1. The live slots of a device come first and number at least 3; among them no value of column 1 appears more than 3 times, and some value exactly 3 times. One device has all 6 slots live.
All inputs are finite; a program needn't handle non-finite values.
Results may differ from the reference program's by a relative error of at most 0.0018.
Values may be sent and summed in bfloat16 or wider, within the bound.
No kernel may reach another device: no remote copies, remote signals or barrier semaphores. Data moves between devices by JAX's collectives and lax.ppermute only.
A program may use at most 64 MiB of HBM per device.

```python
import jax
import jax.numpy as jnp
from jax import lax

CLUSTER_PATCHES = 2048
EXC = 32
DEL = 4
SM = 3
STEPS = 4
INDEX_CLUSTERS = 2
SLOTS_PER_INDEX = 6
GROUPS = 8
NCL = 16
TOTAL_SLOTS = 48


def draw_pair_list(key, part):
    full_key, device_key = jax.random.split(jax.random.fold_in(key, 7))
    full_device = jax.random.randint(full_key, (), 0, GROUPS)

    def one_device(index):
        keys = jax.random.split(jax.random.fold_in(device_key, index), 6)
        lowest = max(SM, SLOTS_PER_INDEX // 4)
        count = jax.random.randint(keys[0], (), lowest, SLOTS_PER_INDEX + 1)
        count = jnp.where(index == full_device, SLOTS_PER_INDEX, count)
        spots = jax.random.permutation(keys[1], GROUPS * SM)
        chosen = jax.random.randint(keys[2], (), 0, GROUPS)
        order = jnp.argsort((spots // SM != chosen).astype(jnp.int32), stable=True)
        owners = (spots[order][:SLOTS_PER_INDEX] // SM).astype(jnp.int32)
        first_local = jax.random.randint(keys[3], (SLOTS_PER_INDEX,), 0, INDEX_CLUSTERS)
        second_local = jax.random.randint(keys[4], (SLOTS_PER_INDEX,), 0, INDEX_CLUSTERS)
        delays = jax.random.randint(keys[5], (SLOTS_PER_INDEX,), 0, DEL)
        live = (jnp.arange(SLOTS_PER_INDEX) < count).astype(jnp.int32)
        return jnp.stack([first_local, owners, second_local, delays, live], axis=1).astype(jnp.int32)
    stacked_tiles = jax.vmap(one_device)(jnp.arange(GROUPS))
    return stacked_tiles.reshape(TOTAL_SLOTS, 5)


def shard_levels(rng, dims, cuts, least, high):
    level = 1.0
    for dim, shards_of in cuts:
        steps = jax.random.uniform(jax.random.fold_in(jax.random.fold_in(rng, 6), dim), (shards_of,), jnp.float32, least / len(cuts), high / len(cuts))
        level = level * jnp.repeat(jnp.exp(steps), dims[dim] // shards_of).reshape((-1,) + (1,) * (len(dims) - 1 - dim))
    return level


def normal_values(key, extent, scale, most, cuts=(), held_as=jnp.bfloat16):
    entries = scale * jax.random.normal(key, extent, jnp.float32)
    if cuts:
        entries = entries * shard_levels(key, extent, cuts, -0.22, 0.18)
    return jnp.clip(entries, -most, most).astype(held_as)


def setup_inputs(seed: int = 0) -> dict:
    streams_of = jax.random.split(jax.random.key(seed), 6)
    pair_list = draw_pair_list(jax.random.fold_in(streams_of[5], 71), 0)
    near_tile_block = normal_values(streams_of[1], (TOTAL_SLOTS, CLUSTER_PATCHES, CLUSTER_PATCHES), (2 * SLOTS_PER_INDEX * CLUSTER_PATCHES // INDEX_CLUSTERS) ** -0.5, 0.0546875, ((0, 8), (2, 4)))
    history = normal_values(streams_of[2], (DEL, NCL, EXC, CLUSTER_PATCHES), 1.0, 6.0, ((1, 8), (3, 4)), jnp.float32)
    excitation = normal_values(streams_of[3], (STEPS, NCL, EXC, CLUSTER_PATCHES), 1.0, 6.0, ((1, 8), (3, 4)), jnp.float32)
    diagonal = jnp.clip(2.0 + 2.0 * jax.random.uniform(streams_of[4], (NCL, CLUSTER_PATCHES), jnp.float32) ** shard_levels(streams_of[4], (NCL, CLUSTER_PATCHES), ((0, 8), (1, 4)), -0.2, 0.2), 2.0, 4.0)
    return dict(pair_list=pair_list, near_tile_block=near_tile_block, history=history, excitation=excitation, diagonal=diagonal)


def reference(pair_list, near_tile_block, history, excitation, diagonal):
    owning_row_list = (jnp.arange(TOTAL_SLOTS) // SLOTS_PER_INDEX).astype(jnp.int32)
    first_cluster = (owning_row_list * INDEX_CLUSTERS + pair_list[:, 0]).astype(jnp.int32)
    second_cluster = (pair_list[:, 1] * INDEX_CLUSTERS + pair_list[:, 2]).astype(jnp.int32)
    delay_index = pair_list[:, 3].astype(jnp.int32)
    weights = pair_list[:, 4].astype(jnp.float32)
    results = []
    for step in range(STEPS):
        rounded = history.astype(jnp.bfloat16)

        def visit(field, item):
            tile, first, second, delay, weight = item
            tile_wide = tile.astype(jnp.float32)
            near_first = rounded[delay, first].astype(jnp.float32)
            near_second = rounded[delay, second].astype(jnp.float32)
            forward = jnp.dot(near_second, tile_wide.T, precision=lax.Precision.HIGHEST)
            backward = jnp.dot(near_first, tile_wide, precision=lax.Precision.HIGHEST)
            field = field.at[first].add(weight * forward)
            field = field.at[second].add(weight * backward)
            return field, None

        start = jnp.zeros((NCL, EXC, CLUSTER_PATCHES), jnp.float32)
        field, unused = lax.scan(visit, start, (near_tile_block, first_cluster, second_cluster, delay_index, weights))
        fresh = (excitation[step] - field) / diagonal[:, None, :]
        results.append(fresh)
        history = jnp.concatenate([fresh[None], history[:-1]], axis=0)
    return jnp.stack(results)
```

```python
import functools

import jax
import jax.numpy as jnp
from jax import lax
from jax.experimental import pallas as pl
from jax.experimental.pallas import tpu as pltpu
from jax.sharding import PartitionSpec as P

STEPS = 4
CORES = 2
F32 = jnp.float32
BF16 = jnp.bfloat16


def swapped(n, bits):
    return [(i, i ^ bits) for i in range(n)]


def far_first(n):
    return sorted(range(1, n), key=lambda k: -bin(k).count("1") * n - k)


def pick(step, delays, slot_delay, slot_cluster, old, new, put):
    for delay in range(delays):

        @pl.when(slot_delay == delay)
        def _(delay=delay):
            if delay < step:
                put([ref[slot_cluster] for ref in new[step - 1 - delay]])
            else:
                put([ref[delay - step, slot_cluster] for ref in old])


def backward_kernel(step, groups, cols, pairs_ref, place_ref, tile_ref, *refs):
    old = refs[:cols]
    new = [refs[cols * (1 + j) : cols * (2 + j)] for j in range(step)]
    same_ref, other_ref, rows_ref, sum_ref = refs[cols * (1 + step) :]
    slots, _, width = tile_ref.shape
    me, col = place_ref[0], place_ref[1]
    sum_ref[...] = jnp.zeros_like(sum_ref)
    for s in range(slots):

        def put(blocks, s=s):
            for k in range(cols):
                rows_ref[s, k] = blocks[k]

        pick(step, old[0].shape[0], pairs_ref[s, 3], pairs_ref[s, 0], old, new, put)
    for s in range(slots):

        @pl.when(pairs_ref[s, 4] == 1)
        def _(s=s):
            total = None
            for k in range(cols):
                start = pl.multiple_of((col ^ k) * width, width)
                part = jnp.dot(
                    rows_ref[s, k],
                    tile_ref[s, pl.ds(start, width), :],
                    preferred_element_type=F32,
                )
                total = part if total is None else total + part
            piece = pairs_ref[s, 1] ^ me
            sum_ref[piece, pairs_ref[s, 2]] += total

    for k in range(groups // CORES):
        same_ref[k] = sum_ref[CORES * k]
        other_ref[k] = sum_ref[CORES * k + 1].astype(other_ref.dtype)


def forward_kernel(step, groups, cols, pairs_ref, place_ref, tile_ref, *refs):
    old = refs[:groups]
    new = [refs[groups * (1 + j) : groups * (2 + j)] for j in range(step)]
    rest = refs[groups * (1 + step) :]
    outs, near_ref, sum_ref = rest[:cols], rest[cols], rest[cols + 1]
    slots, _, width = tile_ref.shape
    me, col = place_ref[0], place_ref[1]
    sum_ref[...] = jnp.zeros_like(sum_ref)
    for s in range(slots):
        piece = pairs_ref[s, 1] ^ me
        for p in range(groups):

            @pl.when(piece == p)
            def _(s=s, p=p):
                def put(blocks):
                    near_ref[s] = blocks[0]

                pick(
                    step,
                    old[0].shape[0],
                    pairs_ref[s, 3],
                    pairs_ref[s, 2],
                    [old[p]],
                    [[n[p]] for n in new],
                    put,
                )

    for s in range(slots):

        @pl.when(pairs_ref[s, 4] == 1)
        def _(s=s):
            for k in range(cols):
                start = pl.multiple_of((col ^ k) * width, width)
                part = lax.dot_general(
                    near_ref[s],
                    tile_ref[s, pl.ds(start, width), :],
                    (((1,), (1,)), ((), ())),
                    preferred_element_type=F32,
                )
                sum_ref[k, pairs_ref[s, 0]] += part

    for k in range(cols):
        outs[k][...] = sum_ref[k].astype(outs[k].dtype)


def shards(pair_list, near_tile_block, history, excitation, diagonal):
    groups = lax.axis_size("pairs")
    cols = lax.axis_size("cols")
    planes = groups // CORES
    delays, clusters, excite, width = history.shape
    slots = pair_list.shape[0]
    block = (clusters, excite, width)
    place = jnp.stack([lax.axis_index("pairs"), lax.axis_index("cols")]).astype(jnp.int32)

    smem = pl.BlockSpec(memory_space=pltpu.SMEM)
    vmem = pl.BlockSpec(memory_space=pltpu.VMEM)
    cost = pl.CostEstimate(
        flops=2 * near_tile_block.size * excite,
        bytes_accessed=2 * near_tile_block.size,
        transcendentals=0,
    )
    limit = pltpu.CompilerParams(vmem_limit_bytes=40 * 2**20)

    def spread_cols(x):
        got = {0: x}
        for k in far_first(cols):
            got[k] = lax.ppermute(x, "cols", swapped(cols, k))
        return [got[k] for k in range(cols)]

    def spread_pairs(x):
        got = {0: x}
        for k in far_first(planes):
            got[CORES * k] = lax.ppermute(x, "pairs", swapped(groups, CORES * k))
        for k in range(planes):
            got[CORES * k + 1] = lax.ppermute(got[CORES * k], "pairs", swapped(groups, 1))
        return [got[p] for p in range(groups)]

    def backward(step, old, new):
        return pl.pallas_call(
            functools.partial(backward_kernel, step, groups, cols),
            out_shape=(
                jax.ShapeDtypeStruct((planes, *block), F32),
                jax.ShapeDtypeStruct((planes, *block), BF16),
            ),
            in_specs=[smem, smem] + [vmem] * (1 + cols * (1 + step)),
            out_specs=(vmem, vmem),
            scratch_shapes=[
                pltpu.VMEM((slots, cols, excite, width), BF16),
                pltpu.VMEM((groups, *block), F32),
            ],
            cost_estimate=cost,
            compiler_params=limit,
            name=f"backward{step}",
        )(pair_list, place, near_tile_block, *old, *[x for n in new for x in n])

    def forward(step, old, new):
        return pl.pallas_call(
            functools.partial(forward_kernel, step, groups, cols),
            out_shape=[jax.ShapeDtypeStruct(block, F32)]
            + [jax.ShapeDtypeStruct(block, BF16)] * (cols - 1),
            in_specs=[smem, smem] + [vmem] * (1 + groups * (1 + step)),
            out_specs=[vmem] * cols,
            scratch_shapes=[
                pltpu.VMEM((slots, excite, width), BF16),
                pltpu.VMEM((cols, *block), F32),
            ],
            cost_estimate=cost,
            compiler_params=limit,
            name=f"forward{step}",
        )(pair_list, place, near_tile_block, *old, *[x for n in new for x in n])

    rounded = history.astype(BF16)
    old_rows = spread_cols(rounded)
    old_near = spread_pairs(rounded)
    new_rows, new_near, results = [], [], []
    for step in range(STEPS):
        same, other = backward(step, old_rows, new_rows)
        mate = lax.ppermute(other, "pairs", swapped(groups, 1))
        field = same[0] + mate[0].astype(F32)
        for k in far_first(planes):
            sent = (same[k] + mate[k].astype(F32)).astype(BF16)
            field += lax.ppermute(sent, "pairs", swapped(groups, CORES * k)).astype(F32)
        parts = forward(step, old_near, new_near)
        field += parts[0]
        for k in far_first(cols):
            field += lax.ppermute(parts[k], "cols", swapped(cols, k)).astype(F32)
        fresh = (excitation[step] - field) / diagonal[:, None, :]
        results.append(fresh)
        if step + 1 < STEPS:
            newest = fresh.astype(BF16)
            new_rows.append(spread_cols(newest))
            new_near.append(spread_pairs(newest))
    return jnp.stack(results)


def solution(mesh):
    placed = (
        P("pairs", None),
        P("pairs", None, "cols"),
        P(None, "pairs", None, "cols"),
        P(None, "pairs", None, "cols"),
        P("pairs", "cols"),
    )
    return jax.shard_map(
        shards,
        mesh=mesh,
        in_specs=placed,
        out_specs=P(None, "pairs", None, "cols"),
        check_vma=False,
    )
```

```python
import functools

import jax
import jax.numpy as jnp
from jax import lax
from jax.experimental import pallas as pl
from jax.experimental.pallas import tpu as pltpu
from jax.sharding import PartitionSpec as P

STEPS = 4
CORES = 2
F32 = jnp.float32
BF16 = jnp.bfloat16


def swapped(n, bits):
    return [(i, i ^ bits) for i in range(n)]


def far_first(n):
    return sorted(range(1, n), key=lambda k: -bin(k).count("1") * n - k)


def pick(step, delays, slot_delay, slot_cluster, old, new, put):
    for delay in range(delays):

        @pl.when(slot_delay == delay)
        def _(delay=delay):
            if delay < step:
                put([ref[slot_cluster] for ref in new[step - 1 - delay]])
            else:
                put([ref[delay - step, slot_cluster] for ref in old])


def turn_kernel(tile_ref, turned_ref):
    slots, rows, width = tile_ref.shape
    part = min(rows, 256)
    for s in range(slots):

        @pl.loop(0, rows // part)
        def _(i, s=s):
            start = pl.multiple_of(i * part, part)
            turned_ref[s, :, pl.ds(start, part)] = tile_ref[s, pl.ds(start, part), :].T


def backward_kernel(step, groups, cols, pairs_ref, place_ref, tile_ref, *refs):
    old = refs[:cols]
    new = [refs[cols * (1 + j) : cols * (2 + j)] for j in range(step)]
    same_ref, other_ref, rows_ref, sum_ref = refs[-4:]
    slots, _, width = tile_ref.shape
    me, col = place_ref[0], place_ref[1]
    sum_ref[...] = jnp.zeros_like(sum_ref)
    for s in range(slots):

        def put(blocks, s=s):
            for k in range(cols):
                start = pl.multiple_of((col ^ k) * width, width)
                rows_ref[s, :, pl.ds(start, width)] = blocks[k]

        pick(step, old[0].shape[0], pairs_ref[s, 3], pairs_ref[s, 0], old, new, put)
    for s in range(slots):

        @pl.when(pairs_ref[s, 4] == 1)
        def _(s=s):
            piece = pairs_ref[s, 1] ^ me
            sum_ref[piece, pairs_ref[s, 2]] += jnp.dot(
                rows_ref[s], tile_ref[s], preferred_element_type=F32
            )

    for k in range(groups // CORES):
        same_ref[k] = sum_ref[CORES * k]
        other_ref[k] = sum_ref[CORES * k + 1].astype(other_ref.dtype)


def forward_kernel(step, groups, cols, pairs_ref, place_ref, turned_ref, *refs):
    old = refs[:groups]
    new = [refs[groups * (1 + j) : groups * (2 + j)] for j in range(step)]
    outs, near_ref, sum_ref = refs[-2 - cols : -2], refs[-2], refs[-1]
    slots, width, _ = turned_ref.shape
    me, col = place_ref[0], place_ref[1]
    sum_ref[...] = jnp.zeros_like(sum_ref)
    for s in range(slots):
        piece = pairs_ref[s, 1] ^ me
        for p in range(groups):

            @pl.when(piece == p)
            def _(s=s, p=p):
                def put(blocks):
                    near_ref[s] = blocks[0]

                pick(
                    step,
                    old[0].shape[0],
                    pairs_ref[s, 3],
                    pairs_ref[s, 2],
                    [old[p]],
                    [[n[p]] for n in new],
                    put,
                )

    for s in range(slots):

        @pl.when(pairs_ref[s, 4] == 1)
        def _(s=s):
            sum_ref[pairs_ref[s, 0]] += jnp.dot(
                near_ref[s], turned_ref[s], preferred_element_type=F32
            )

    for k in range(cols):
        start = pl.multiple_of((col ^ k) * width, width)
        outs[k][...] = sum_ref[:, :, pl.ds(start, width)].astype(outs[k].dtype)


def shards(pair_list, near_tile_block, history, excitation, diagonal):
    groups = lax.axis_size("pairs")
    cols = lax.axis_size("cols")
    planes = groups // CORES
    delays, clusters, excite, width = history.shape
    slots = pair_list.shape[0]
    block = (clusters, excite, width)
    place = jnp.stack([lax.axis_index("pairs"), lax.axis_index("cols")]).astype(jnp.int32)

    smem = pl.BlockSpec(memory_space=pltpu.SMEM)
    vmem = pl.BlockSpec(memory_space=pltpu.VMEM)
    anywhere = pl.BlockSpec(memory_space=pl.ANY)
    rows = near_tile_block.shape[1]
    cost = pl.CostEstimate(
        flops=2 * near_tile_block.size * excite,
        bytes_accessed=2 * near_tile_block.size,
        transcendentals=0,
    )
    limit = pltpu.CompilerParams(vmem_limit_bytes=16 * 2**20)
    turned = pl.pallas_call(
        turn_kernel,
        out_shape=pltpu.VMEM((slots, width, rows), BF16),
        in_specs=[vmem],
        out_specs=vmem,
        cost_estimate=cost,
        compiler_params=limit,
        name="turn",
    )(near_tile_block)

    def spread_cols(x):
        got = {0: x}
        for k in far_first(cols):
            got[k] = lax.ppermute(x, "cols", swapped(cols, k))
        return [got[k] for k in range(cols)]

    def spread_pairs(x, before=None):
        got = {0: x}
        for k in far_first(planes):
            got[CORES * k] = lax.ppermute(x, "pairs", swapped(groups, CORES * k))
        if before is not None:
            got, before = lax.optimization_barrier((got, before))
        for k in range(planes):
            got[CORES * k + 1] = lax.ppermute(got[CORES * k], "pairs", swapped(groups, 1))
        got = [got[p] for p in range(groups)]
        return got if before is None else (got, before)

    def backward(step, old, new, after):
        return pl.pallas_call(
            functools.partial(backward_kernel, step, groups, cols),
            out_shape=(
                jax.ShapeDtypeStruct((planes, *block), F32),
                jax.ShapeDtypeStruct((planes, *block), BF16),
            ),
            in_specs=[smem, smem]
            + [vmem] * (1 + cols * (1 + step))
            + [anywhere] * len(after),
            out_specs=(vmem, vmem),
            scratch_shapes=[
                pltpu.VMEM((slots, excite, rows), BF16),
                pltpu.VMEM((groups, *block), F32),
            ],
            cost_estimate=cost,
            compiler_params=limit,
            name=f"backward{step}",
        )(pair_list, place, near_tile_block, *old, *[x for n in new for x in n], *after)

    def forward(step, old, new, after):
        return pl.pallas_call(
            functools.partial(forward_kernel, step, groups, cols),
            out_shape=[jax.ShapeDtypeStruct(block, F32)]
            + [jax.ShapeDtypeStruct(block, BF16)] * (cols - 1),
            in_specs=[smem, smem]
            + [vmem] * (1 + groups * (1 + step))
            + [anywhere] * len(after),
            out_specs=[vmem] * cols,
            scratch_shapes=[
                pltpu.VMEM((slots, excite, width), BF16),
                pltpu.VMEM((clusters, excite, rows), F32),
            ],
            cost_estimate=cost,
            compiler_params=limit,
            name=f"forward{step}",
        )(pair_list, place, turned, *old, *[x for n in new for x in n], *after)

    rounded = history.astype(BF16)
    old_rows = spread_cols(rounded)
    old_near, turned = spread_pairs(rounded, turned)
    new_rows, new_near, results = [], [], []
    for step in range(STEPS):
        same, other = backward(step, old_rows, new_rows, new_near[-1][::CORES] if step else [])
        mate = lax.ppermute(other, "pairs", swapped(groups, 1))
        field = same[0] + mate[0].astype(F32)
        for k in far_first(planes):
            sent = (same[k] + mate[k].astype(F32)).astype(BF16)
            field += lax.ppermute(sent, "pairs", swapped(groups, CORES * k)).astype(F32)
        parts = forward(step, old_near, new_near, [same])
        field += parts[0]
        for k in far_first(cols):
            field += lax.ppermute(parts[k], "cols", swapped(cols, k)).astype(F32)
        fresh = (excitation[step] - field) / diagonal[:, None, :]
        results.append(fresh)
        if step + 1 < STEPS:
            newest = fresh.astype(BF16)
            new_rows.append(spread_cols(newest))
            new_near.append(spread_pairs(newest))
    return jnp.stack(results)


def solution(mesh):
    placed = (
        P("pairs", None),
        P("pairs", None, "cols"),
        P(None, "pairs", None, "cols"),
        P(None, "pairs", None, "cols"),
        P("pairs", "cols"),
    )
    return jax.shard_map(
        shards,
        mesh=mesh,
        in_specs=placed,
        out_specs=P(None, "pairs", None, "cols"),
        check_vma=False,
    )
```

```python
import functools

import jax
import jax.numpy as jnp
from jax import lax
from jax.experimental import pallas as pl
from jax.experimental.pallas import tpu as pltpu
from jax.sharding import PartitionSpec as P

STEPS = 4
CORES = 2
F32 = jnp.float32
BF16 = jnp.bfloat16


def swapped(n, bits):
    return [(i, i ^ bits) for i in range(n)]


def far_first(n):
    return sorted(range(1, n), key=lambda k: -bin(k).count("1") * n - k)


def pick(step, delays, slot_delay, slot_cluster, old, new, put):
    for delay in range(delays):

        @pl.when(slot_delay == delay)
        def _(delay=delay):
            if delay < step:
                put([ref[slot_cluster] for ref in new[step - 1 - delay]])
            else:
                put([ref[delay - step, slot_cluster] for ref in old])


def turn_kernel(tile_ref, turned_ref):
    slots, rows, width = tile_ref.shape
    part = min(rows, 256)
    for s in range(slots):

        @pl.loop(0, rows // part)
        def _(i, s=s):
            start = pl.multiple_of(i * part, part)
            turned_ref[s, :, pl.ds(start, part)] = tile_ref[s, pl.ds(start, part), :].T


def backward_kernel(step, groups, cols, pairs_ref, place_ref, tile_ref, *refs):
    old = refs[:cols]
    new = [refs[cols * (1 + j) : cols * (2 + j)] for j in range(step)]
    same_ref, other_ref, rows_ref, sum_ref = refs[-4:]
    slots, _, width = tile_ref.shape
    me, col = place_ref[0], place_ref[1]
    sum_ref[...] = jnp.zeros_like(sum_ref)
    for s in range(slots):

        def put(blocks, s=s):
            for k in range(cols):
                start = pl.multiple_of((col ^ k) * width, width)
                rows_ref[s, :, pl.ds(start, width)] = blocks[k]

        pick(step, old[0].shape[0], pairs_ref[s, 3], pairs_ref[s, 0], old, new, put)
    for s in range(slots):

        @pl.when(pairs_ref[s, 4] == 1)
        def _(s=s):
            piece = pairs_ref[s, 1] ^ me
            sum_ref[piece, pairs_ref[s, 2]] += jnp.dot(
                rows_ref[s], tile_ref[s], preferred_element_type=F32
            )

    for k in range(groups // CORES):
        same_ref[k] = sum_ref[CORES * k]
        other_ref[k] = sum_ref[CORES * k + 1].astype(other_ref.dtype)


def forward_kernel(step, groups, cols, pairs_ref, place_ref, turned_ref, *refs):
    old = refs[:groups]
    new = [refs[groups * (1 + j) : groups * (2 + j)] for j in range(step)]
    outs, near_ref, sum_ref = refs[-2 - cols : -2], refs[-2], refs[-1]
    slots, width, _ = turned_ref.shape
    me, col = place_ref[0], place_ref[1]
    sum_ref[...] = jnp.zeros_like(sum_ref)
    for s in range(slots):
        piece = pairs_ref[s, 1] ^ me
        for p in range(groups):

            @pl.when(piece == p)
            def _(s=s, p=p):
                def put(blocks):
                    near_ref[s] = blocks[0]

                pick(
                    step,
                    old[0].shape[0],
                    pairs_ref[s, 3],
                    pairs_ref[s, 2],
                    [old[p]],
                    [[n[p]] for n in new],
                    put,
                )

    for s in range(slots):

        @pl.when(pairs_ref[s, 4] == 1)
        def _(s=s):
            sum_ref[pairs_ref[s, 0]] += jnp.dot(
                near_ref[s], turned_ref[s], preferred_element_type=F32
            )

    for k in range(cols):
        start = pl.multiple_of((col ^ k) * width, width)
        outs[k][...] = sum_ref[:, :, pl.ds(start, width)].astype(outs[k].dtype)


def shards(pair_list, near_tile_block, history, excitation, diagonal):
    groups = lax.axis_size("pairs")
    cols = lax.axis_size("cols")
    planes = groups // CORES
    delays, clusters, excite, width = history.shape
    slots = pair_list.shape[0]
    block = (clusters, excite, width)
    place = jnp.stack([lax.axis_index("pairs"), lax.axis_index("cols")]).astype(jnp.int32)

    smem = pl.BlockSpec(memory_space=pltpu.SMEM)
    vmem = pl.BlockSpec(memory_space=pltpu.VMEM)
    anywhere = pl.BlockSpec(memory_space=pl.ANY)
    rows = near_tile_block.shape[1]
    cost = pl.CostEstimate(
        flops=2 * near_tile_block.size * excite,
        bytes_accessed=2 * near_tile_block.size,
        transcendentals=0,
    )
    limit = pltpu.CompilerParams(vmem_limit_bytes=16 * 2**20)
    turned = pl.pallas_call(
        turn_kernel,
        out_shape=pltpu.VMEM((slots, width, rows), BF16),
        in_specs=[vmem],
        out_specs=vmem,
        cost_estimate=cost,
        compiler_params=limit,
        name="turn",
    )(near_tile_block)

    def spread_cols(x):
        got = {0: x}
        for k in far_first(cols):
            got[k] = lax.ppermute(x, "cols", swapped(cols, k))
        return [got[k] for k in range(cols)]

    def spread_planes(x):
        got = {0: x}
        for k in far_first(planes):
            got[k] = lax.ppermute(x, "pairs", swapped(groups, CORES * k))
        return [got[k] for k in range(planes)]

    def spread_cores(xs):
        return [y for x in xs for y in (x, lax.ppermute(x, "pairs", swapped(groups, 1)))]

    def backward(step, old, new):
        return pl.pallas_call(
            functools.partial(backward_kernel, step, groups, cols),
            out_shape=(
                jax.ShapeDtypeStruct((planes, *block), F32),
                jax.ShapeDtypeStruct((planes, *block), BF16),
            ),
            in_specs=[smem, smem]
            + [vmem] * (1 + cols * (1 + step)),
            out_specs=(vmem, vmem),
            scratch_shapes=[
                pltpu.VMEM((slots, excite, rows), BF16),
                pltpu.VMEM((groups, *block), F32),
            ],
            cost_estimate=cost,
            compiler_params=limit,
            name=f"backward{step}",
        )(pair_list, place, near_tile_block, *old, *[x for n in new for x in n])

    def forward(step, old, new, after):
        return pl.pallas_call(
            functools.partial(forward_kernel, step, groups, cols),
            out_shape=[jax.ShapeDtypeStruct(block, F32)]
            + [jax.ShapeDtypeStruct(block, BF16)] * (cols - 1),
            in_specs=[smem, smem]
            + [vmem] * (1 + groups * (1 + step))
            + [anywhere] * len(after),
            out_specs=[vmem] * cols,
            scratch_shapes=[
                pltpu.VMEM((slots, excite, width), BF16),
                pltpu.VMEM((clusters, excite, rows), F32),
            ],
            cost_estimate=cost,
            compiler_params=limit,
            name=f"forward{step}",
        )(pair_list, place, turned, *old, *[x for n in new for x in n], *after)

    rounded = history.astype(BF16)
    planes_next = spread_planes(rounded)
    cols_next = spread_cols(rounded)
    rows_of, near_of, results = [], [], []
    for step in range(STEPS):
        rows_of.append(cols_next)
        same, other = backward(step, rows_of[0], rows_of[1:])
        if step == 0:
            planes_next, same, turned = lax.optimization_barrier((planes_next, same, turned))
        else:
            planes_next, same, other = lax.optimization_barrier((planes_next, same, other))
        mate = lax.ppermute(other, "pairs", swapped(groups, 1))
        near_of.append(spread_cores(planes_next))
        sent = [same[k] + mate[k].astype(F32) for k in range(planes)]
        sent[1:] = [x.astype(BF16) for x in sent[1:]]
        field = sent[0]
        for k in far_first(planes):
            field += lax.ppermute(sent[k], "pairs", swapped(groups, CORES * k)).astype(F32)
        parts = forward(step, near_of[0], near_of[1:], sent)
        field += parts[0]
        for k in far_first(cols):
            field += lax.ppermute(parts[k], "cols", swapped(cols, k)).astype(F32)
        fresh = (excitation[step] - field) / diagonal[:, None, :]
        results.append(fresh)
        if step + 1 < STEPS:
            newest = fresh.astype(BF16)
            planes_next = spread_planes(newest)
            cols_next = spread_cols(newest)
    return jnp.stack(results)


def solution(mesh):
    placed = (
        P("pairs", None),
        P("pairs", None, "cols"),
        P(None, "pairs", None, "cols"),
        P(None, "pairs", None, "cols"),
        P("pairs", "cols"),
    )
    return jax.shard_map(
        shards,
        mesh=mesh,
        in_specs=placed,
        out_specs=P(None, "pairs", None, "cols"),
        check_vma=False,
    )
```

```python
import functools

import jax
import jax.numpy as jnp
from jax import lax
from jax.experimental import pallas as pl
from jax.experimental.pallas import tpu as pltpu
from jax.sharding import PartitionSpec as P

STEPS = 4
CORES = 2
F32 = jnp.float32
BF16 = jnp.bfloat16


def swapped(n, bits):
    return [(i, i ^ bits) for i in range(n)]


def far_first(n):
    return sorted(range(1, n), key=lambda k: -bin(k).count("1") * n - k)


FIRST, PIECE, SECOND, DELAY, LIVE = range(5)


def table_kernel(pairs_ref, table_ref):
    slots = pairs_ref.shape[0]
    me, col = lax.axis_index("pairs"), lax.axis_index("cols")
    for s in range(slots):
        for i in range(5):
            value = pairs_ref[s, i]
            table_ref[s, i] = value ^ me if i == PIECE else value
    for i in range(5):
        table_ref[slots, i] = col


def pick(step, table_ref, s, old, new, put):
    live = table_ref[s, LIVE] == 1
    delay = table_ref[s, DELAY]

    def zero_dead(blocks):
        put([jnp.where(live, x, jnp.zeros_like(x)) for x in blocks])

    for j in range(step):

        @pl.when(delay == j)
        def _(j=j):
            zero_dead(new(step - 1 - j))

    @pl.when(delay >= step)
    def _():
        zero_dead(old(delay - step))


def turn_kernel(tile_ref, turned_ref):
    slots, rows, width = tile_ref.shape
    part = min(rows, 256)
    for s in range(slots):

        @pl.loop(0, rows // part)
        def _(i, s=s):
            start = pl.multiple_of(i * part, part)
            turned_ref[s, :, pl.ds(start, part)] = tile_ref[s, pl.ds(start, part), :].T


def backward_kernel(step, groups, cols, table_ref, tile_ref, *refs):
    old = refs[:cols]
    new = [refs[cols * (1 + j) : cols * (2 + j)] for j in range(step)]
    same_ref, other_ref, rows_ref, sum_ref = refs[-4:]
    slots, _, width = tile_ref.shape
    col = table_ref[slots, 0]
    sum_ref[...] = jnp.zeros_like(sum_ref)
    for s in range(slots):

        def put(blocks, s=s):
            for k in range(cols):
                start = pl.multiple_of((col ^ k) * width, width)
                rows_ref[s, :, pl.ds(start, width)] = blocks[k]

        first = table_ref[s, FIRST]
        pick(
            step,
            table_ref,
            s,
            lambda d, first=first: [ref[d, first] for ref in old],
            lambda j, first=first: [ref[first] for ref in new[j]],
            put,
        )
    for s in range(slots):
        sum_ref[table_ref[s, PIECE], table_ref[s, SECOND]] += jnp.dot(
            rows_ref[s], tile_ref[s], preferred_element_type=F32
        )

    for k in range(groups // CORES):
        same_ref[k] = sum_ref[CORES * k]
        other_ref[k] = sum_ref[CORES * k + 1].astype(other_ref.dtype)


def forward_kernel(step, groups, cols, table_ref, turned_ref, *refs):
    old = refs[:groups]
    new = [refs[groups * (1 + j) : groups * (2 + j)] for j in range(step)]
    outs, near_ref, sum_ref = refs[-2 - cols : -2], refs[-2], refs[-1]
    slots, width, _ = turned_ref.shape
    col = table_ref[slots, 0]
    sum_ref[...] = jnp.zeros_like(sum_ref)
    for s in range(slots):

        def put(blocks, s=s):
            near_ref[s] = blocks[0]

        second = table_ref[s, SECOND]
        for p in range(groups):

            @pl.when(table_ref[s, PIECE] == p)
            def _(s=s, p=p, second=second, put=put):
                pick(
                    step,
                    table_ref,
                    s,
                    lambda d: [old[p][d, second]],
                    lambda j: [new[j][p][second]],
                    put,
                )

    for s in range(slots):
        sum_ref[table_ref[s, FIRST]] += jnp.dot(
            near_ref[s], turned_ref[s], preferred_element_type=F32
        )

    for k in range(cols):
        start = pl.multiple_of((col ^ k) * width, width)
        outs[k][...] = sum_ref[:, :, pl.ds(start, width)].astype(outs[k].dtype)


def shards(pair_list, near_tile_block, history, excitation, diagonal):
    groups = lax.axis_size("pairs")
    cols = lax.axis_size("cols")
    planes = groups // CORES
    delays, clusters, excite, width = history.shape
    slots = pair_list.shape[0]
    block = (clusters, excite, width)

    smem = pl.BlockSpec(memory_space=pltpu.SMEM)
    vmem = pl.BlockSpec(memory_space=pltpu.VMEM)
    anywhere = pl.BlockSpec(memory_space=pl.ANY)
    rows = near_tile_block.shape[1]
    cost = pl.CostEstimate(
        flops=2 * near_tile_block.size * excite,
        bytes_accessed=2 * near_tile_block.size,
        transcendentals=0,
    )
    limit = pltpu.CompilerParams(vmem_limit_bytes=16 * 2**20)
    table = pl.pallas_call(
        table_kernel,
        out_shape=pltpu.SMEM((slots + 1, 5), jnp.int32),
        in_specs=[smem],
        out_specs=smem,
        compiler_params=pltpu.CompilerParams(vmem_limit_bytes=2**20),
        name="table",
    )(pair_list)
    def spread_cols(x):
        got = {0: x}
        for k in far_first(cols):
            got[k] = lax.ppermute(x, "cols", swapped(cols, k))
        return [got[k] for k in range(cols)]

    def spread_planes(x):
        got = {0: x}
        for k in far_first(planes):
            got[k] = lax.ppermute(x, "pairs", swapped(groups, CORES * k))
        return [got[k] for k in range(planes)]

    def spread_cores(xs):
        return [y for x in xs for y in (x, lax.ppermute(x, "pairs", swapped(groups, 1)))]

    def backward(step, old, new):
        return pl.pallas_call(
            functools.partial(backward_kernel, step, groups, cols),
            out_shape=(
                jax.ShapeDtypeStruct((planes, *block), F32),
                jax.ShapeDtypeStruct((planes, *block), BF16),
            ),
            in_specs=[smem]
            + [vmem] * (1 + cols * (1 + step)),
            out_specs=(vmem, vmem),
            scratch_shapes=[
                pltpu.VMEM((slots, excite, rows), BF16),
                pltpu.VMEM((groups, *block), F32),
            ],
            cost_estimate=cost,
            compiler_params=limit,
            name=f"backward{step}",
        )(table, near_tile_block, *old, *[x for n in new for x in n])

    def forward(step, old, new, after):
        return pl.pallas_call(
            functools.partial(forward_kernel, step, groups, cols),
            out_shape=[jax.ShapeDtypeStruct(block, F32)]
            + [jax.ShapeDtypeStruct(block, BF16)] * (cols - 1),
            in_specs=[smem]
            + [vmem] * (1 + groups * (1 + step))
            + [anywhere] * len(after),
            out_specs=[vmem] * cols,
            scratch_shapes=[
                pltpu.VMEM((slots, excite, width), BF16),
                pltpu.VMEM((clusters, excite, rows), F32),
            ],
            cost_estimate=cost,
            compiler_params=limit,
            name=f"forward{step}",
        )(table, turned, *old, *[x for n in new for x in n], *after)

    rounded = history.astype(BF16)
    planes_next = spread_planes(rounded)
    cols_next = spread_cols(rounded)
    cols_next[-1], tile = lax.optimization_barrier((cols_next[-1], near_tile_block))
    turned = pl.pallas_call(
        turn_kernel,
        out_shape=pltpu.VMEM((slots, width, rows), BF16),
        in_specs=[vmem],
        out_specs=vmem,
        cost_estimate=cost,
        compiler_params=limit,
        name="turn",
    )(tile)
    rows_of, near_of, results = [], [], []
    for step in range(STEPS):
        if step == 0:
            cols_next, turned, table = lax.optimization_barrier((cols_next, turned, table))
        rows_of.append(cols_next)
        same, other = backward(step, rows_of[0], rows_of[1:])
        if step:
            planes_next, same, other = lax.optimization_barrier((planes_next, same, other))
        mate = lax.ppermute(other, "pairs", swapped(groups, 1))
        near_of.append(spread_cores(planes_next))
        sent = [same[k] + mate[k].astype(F32) for k in range(planes)]
        sent[1:] = [x.astype(BF16) for x in sent[1:]]
        field = sent[0]
        for k in far_first(planes):
            field += lax.ppermute(sent[k], "pairs", swapped(groups, CORES * k)).astype(F32)
        parts = forward(step, near_of[0], near_of[1:], sent)
        field += parts[0]
        for k in far_first(cols):
            field += lax.ppermute(parts[k], "cols", swapped(cols, k)).astype(F32)
        fresh = (excitation[step] - field) / diagonal[:, None, :]
        results.append(fresh)
        if step + 1 < STEPS:
            newest = fresh.astype(BF16)
            planes_next = spread_planes(newest)
            cols_next = spread_cols(newest)
    return jnp.stack(results)


def solution(mesh):
    placed = (
        P("pairs", None),
        P("pairs", None, "cols"),
        P(None, "pairs", None, "cols"),
        P(None, "pairs", None, "cols"),
        P("pairs", "cols"),
    )
    return jax.shard_map(
        shards,
        mesh=mesh,
        in_specs=placed,
        out_specs=P(None, "pairs", None, "cols"),
        check_vma=False,
    )
```

```python
import functools

import jax
import jax.numpy as jnp
from jax import lax
from jax.experimental import pallas as pl
from jax.experimental.pallas import tpu as pltpu
from jax.sharding import PartitionSpec as P

STEPS = 4
CORES = 2
F32 = jnp.float32
BF16 = jnp.bfloat16


def swapped(n, bits):
    return [(i, i ^ bits) for i in range(n)]


def far_first(n):
    return sorted(range(1, n), key=lambda k: -bin(k).count("1") * n - k)


FIRST, PIECE, SECOND, DELAY, LIVE = range(5)


def table_kernel(pairs_ref, table_ref):
    slots = pairs_ref.shape[0]
    me, col = lax.axis_index("pairs"), lax.axis_index("cols")
    for s in range(slots):
        for i in range(5):
            value = pairs_ref[s, i]
            table_ref[s, i] = value ^ me if i == PIECE else value
    for i in range(5):
        table_ref[slots, i] = col


def choose(index, low, high, do):
    if high - low == 1:
        do(low)
        return
    middle = (low + high) // 2
    lax.cond(
        index < middle,
        lambda: choose(index, low, middle, do),
        lambda: choose(index, middle, high, do),
    )


def pick(step, table_ref, s, old, new, put):
    live = table_ref[s, LIVE] == 1
    delay = table_ref[s, DELAY]

    def zero_dead(blocks):
        put([jnp.where(live, x, jnp.zeros_like(x)) for x in blocks])

    def from_step(j):
        zero_dead(new(step - 1 - j) if j < step else old(delay - step))

    choose(jnp.minimum(delay, step), 0, step + 1, from_step)


def turn_kernel(tile_ref, turned_ref):
    slots, rows, width = tile_ref.shape
    part = min(rows, 256)
    for s in range(slots):

        @pl.loop(0, rows // part)
        def _(i, s=s):
            start = pl.multiple_of(i * part, part)
            turned_ref[s, :, pl.ds(start, part)] = tile_ref[s, pl.ds(start, part), :].T


def backward_kernel(step, groups, cols, table_ref, tile_ref, *refs):
    old = refs[:cols]
    new = [refs[cols * (1 + j) : cols * (2 + j)] for j in range(step)]
    same_ref, other_ref, rows_ref, sum_ref = refs[-4:]
    slots, _, width = tile_ref.shape
    col = table_ref[slots, 0]
    sum_ref[...] = jnp.zeros_like(sum_ref)
    for s in range(slots):

        def put(blocks, s=s):
            for k in range(cols):
                start = pl.multiple_of((col ^ k) * width, width)
                rows_ref[s, :, pl.ds(start, width)] = blocks[k]

        first = table_ref[s, FIRST]
        pick(
            step,
            table_ref,
            s,
            lambda d, first=first: [ref[d, first] for ref in old],
            lambda j, first=first: [ref[first] for ref in new[j]],
            put,
        )
    for s in range(slots):
        sum_ref[table_ref[s, PIECE], table_ref[s, SECOND]] += jnp.dot(
            rows_ref[s], tile_ref[s], preferred_element_type=F32
        )

    for k in range(groups // CORES):
        same_ref[k] = sum_ref[CORES * k]
        other_ref[k] = sum_ref[CORES * k + 1].astype(other_ref.dtype)


def forward_kernel(step, groups, cols, table_ref, turned_ref, *refs):
    old = refs[:groups]
    new = [refs[groups * (1 + j) : groups * (2 + j)] for j in range(step)]
    outs, near_ref, sum_ref = refs[-2 - cols : -2], refs[-2], refs[-1]
    slots, width, _ = turned_ref.shape
    col = table_ref[slots, 0]
    sum_ref[...] = jnp.zeros_like(sum_ref)
    for s in range(slots):

        def put(blocks, s=s):
            near_ref[s] = blocks[0]

        second = table_ref[s, SECOND]

        def from_piece(p, s=s, second=second, put=put):
            pick(
                step,
                table_ref,
                s,
                lambda d: [old[p][d, second]],
                lambda j: [new[j][p][second]],
                put,
            )

        choose(table_ref[s, PIECE], 0, groups, from_piece)

    for s in range(slots):
        sum_ref[table_ref[s, FIRST]] += jnp.dot(
            near_ref[s], turned_ref[s], preferred_element_type=F32
        )

    for k in range(cols):
        start = pl.multiple_of((col ^ k) * width, width)
        outs[k][...] = sum_ref[:, :, pl.ds(start, width)].astype(outs[k].dtype)


def shards(pair_list, near_tile_block, history, excitation, diagonal):
    groups = lax.axis_size("pairs")
    cols = lax.axis_size("cols")
    planes = groups // CORES
    delays, clusters, excite, width = history.shape
    slots = pair_list.shape[0]
    block = (clusters, excite, width)

    smem = pl.BlockSpec(memory_space=pltpu.SMEM)
    vmem = pl.BlockSpec(memory_space=pltpu.VMEM)
    anywhere = pl.BlockSpec(memory_space=pl.ANY)
    rows = near_tile_block.shape[1]
    cost = pl.CostEstimate(
        flops=2 * near_tile_block.size * excite,
        bytes_accessed=2 * near_tile_block.size,
        transcendentals=0,
    )
    limit = pltpu.CompilerParams(vmem_limit_bytes=16 * 2**20)
    table = pl.pallas_call(
        table_kernel,
        out_shape=pltpu.SMEM((slots + 1, 5), jnp.int32),
        in_specs=[smem],
        out_specs=smem,
        compiler_params=pltpu.CompilerParams(vmem_limit_bytes=2**20),
        name="table",
    )(pair_list)
    def spread_cols(x):
        got = {0: x}
        for k in far_first(cols):
            got[k] = lax.ppermute(x, "cols", swapped(cols, k))
        return [got[k] for k in range(cols)]

    def spread_planes(x):
        got = {0: x}
        for k in far_first(planes):
            got[k] = lax.ppermute(x, "pairs", swapped(groups, CORES * k))
        return [got[k] for k in range(planes)]

    def spread_cores(xs):
        return [y for x in xs for y in (x, lax.ppermute(x, "pairs", swapped(groups, 1)))]

    def backward(step, old, new):
        return pl.pallas_call(
            functools.partial(backward_kernel, step, groups, cols),
            out_shape=(
                jax.ShapeDtypeStruct((planes, *block), F32),
                jax.ShapeDtypeStruct((planes, *block), BF16),
            ),
            in_specs=[smem]
            + [vmem] * (1 + cols * (1 + step)),
            out_specs=(vmem, vmem),
            scratch_shapes=[
                pltpu.VMEM((slots, excite, rows), BF16),
                pltpu.VMEM((groups, *block), F32),
            ],
            cost_estimate=cost,
            compiler_params=limit,
            name=f"backward{step}",
        )(table, near_tile_block, *old, *[x for n in new for x in n])

    def forward(step, old, new, after):
        return pl.pallas_call(
            functools.partial(forward_kernel, step, groups, cols),
            out_shape=[jax.ShapeDtypeStruct(block, F32)]
            + [jax.ShapeDtypeStruct(block, BF16)] * (cols - 1),
            in_specs=[smem]
            + [vmem] * (1 + groups * (1 + step))
            + [anywhere] * len(after),
            out_specs=[vmem] * cols,
            scratch_shapes=[
                pltpu.VMEM((slots, excite, width), BF16),
                pltpu.VMEM((clusters, excite, rows), F32),
            ],
            cost_estimate=cost,
            compiler_params=limit,
            name=f"forward{step}",
        )(table, turned, *old, *[x for n in new for x in n], *after)

    rounded = history.astype(BF16)
    planes_next = spread_planes(rounded)
    cols_next = spread_cols(rounded)
    cols_next[-1], tile = lax.optimization_barrier((cols_next[-1], near_tile_block))
    turned = pl.pallas_call(
        turn_kernel,
        out_shape=pltpu.VMEM((slots, width, rows), BF16),
        in_specs=[vmem],
        out_specs=vmem,
        cost_estimate=cost,
        compiler_params=limit,
        name="turn",
    )(tile)
    rows_of, near_of, results = [], [], []
    for step in range(STEPS):
        if step == 0:
            cols_next, planes_next[-1], turned, table = lax.optimization_barrier((cols_next, planes_next[-1], turned, table))
        rows_of.append(cols_next)
        same, other = backward(step, rows_of[0], rows_of[1:])
        if step:
            planes_next, same, other = lax.optimization_barrier((planes_next, same, other))
        mate = lax.ppermute(other, "pairs", swapped(groups, 1))
        near_of.append(spread_cores(planes_next))
        sent = [same[k] + mate[k].astype(F32) for k in range(planes)]
        sent[1:] = [x.astype(BF16) for x in sent[1:]]
        field = sent[0]
        for k in far_first(planes):
            field += lax.ppermute(sent[k], "pairs", swapped(groups, CORES * k)).astype(F32)
        parts = forward(step, near_of[0], near_of[1:], sent)
        field += parts[0]
        for k in far_first(cols):
            field += lax.ppermute(parts[k], "cols", swapped(cols, k)).astype(F32)
        fresh = (excitation[step] - field) / diagonal[:, None, :]
        results.append(fresh)
        if step + 1 < STEPS:
            newest = fresh.astype(BF16)
            planes_next = spread_planes(newest)
            cols_next = spread_cols(newest)
    return jnp.stack(results)


def solution(mesh):
    placed = (
        P("pairs", None),
        P("pairs", None, "cols"),
        P(None, "pairs", None, "cols"),
        P(None, "pairs", None, "cols"),
        P("pairs", "cols"),
    )
    return jax.shard_map(
        shards,
        mesh=mesh,
        in_specs=placed,
        out_specs=P(None, "pairs", None, "cols"),
        check_vma=False,
    )
```

```python
import functools

import jax
import jax.numpy as jnp
from jax import lax
from jax.experimental import pallas as pl
from jax.experimental.pallas import tpu as pltpu
from jax.sharding import PartitionSpec as P

STEPS = 4
CORES = 2
F32 = jnp.float32
BF16 = jnp.bfloat16


def swapped(n, bits):
    return [(i, i ^ bits) for i in range(n)]


def far_first(n):
    return sorted(range(1, n), key=lambda k: -bin(k).count("1") * n - k)


FIRST, PIECE, SECOND, DELAY, LIVE = range(5)


def table_kernel(pairs_ref, table_ref):
    slots = pairs_ref.shape[0]
    me, col = lax.axis_index("pairs"), lax.axis_index("cols")
    for s in range(slots):
        for i in range(5):
            value = pairs_ref[s, i]
            table_ref[s, i] = value ^ me if i == PIECE else value
    for i in range(5):
        table_ref[slots, i] = col


def choose(index, low, high, do):
    if high - low == 1:
        do(low)
        return
    middle = (low + high) // 2
    lax.cond(
        index < middle,
        lambda: choose(index, low, middle, do),
        lambda: choose(index, middle, high, do),
    )


def pick(step, table_ref, s, old, new, put):
    live = table_ref[s, LIVE] == 1
    delay = table_ref[s, DELAY]

    def zero_dead(blocks):
        put([jnp.where(live, x, jnp.zeros_like(x)) for x in blocks])

    def from_step(j):
        zero_dead(new(step - 1 - j) if j < step else old(delay - step))

    choose(jnp.minimum(delay, step), 0, step + 1, from_step)


def turn_kernel(tile_ref, turned_ref):
    slots, rows, width = tile_ref.shape
    part = min(rows, 256)
    for s in range(slots):

        @pl.loop(0, rows // part)
        def _(i, s=s):
            start = pl.multiple_of(i * part, part)
            turned_ref[s, :, pl.ds(start, part)] = tile_ref[s, pl.ds(start, part), :].T


def backward_kernel(step, groups, cols, table_ref, tile_ref, *refs):
    old = refs[:cols]
    new = [refs[cols * (1 + j) : cols * (2 + j)] for j in range(step)]
    same_ref, other_ref, rows_ref, sum_ref = refs[-4:]
    slots, _, width = tile_ref.shape
    col = table_ref[slots, 0]
    sum_ref[...] = jnp.zeros_like(sum_ref)
    for s in range(slots):

        def put(blocks, s=s):
            for k in range(cols):
                start = pl.multiple_of((col ^ k) * width, width)
                rows_ref[s, :, pl.ds(start, width)] = blocks[k]

        first = table_ref[s, FIRST]
        pick(
            step,
            table_ref,
            s,
            lambda d, first=first: [ref[d, first] for ref in old],
            lambda j, first=first: [ref[first] for ref in new[j]],
            put,
        )
    for s in range(slots):
        sum_ref[table_ref[s, PIECE], table_ref[s, SECOND]] += jnp.dot(
            rows_ref[s], tile_ref[s], preferred_element_type=F32
        )

    for k in range(groups // CORES):
        same_ref[k] = sum_ref[CORES * k]
        other_ref[k] = sum_ref[CORES * k + 1].astype(other_ref.dtype)


def forward_kernel(step, groups, cols, table_ref, turned_ref, *refs):
    planes = groups // CORES
    old, new = refs[:groups], []
    for j in range(step):
        first = groups + (planes + 1) * j
        mates = refs[first + planes]
        new.append([r for k in range(planes) for r in (refs[first + k], mates.at[k])])
    outs, near_ref, sum_ref = refs[-2 - cols : -2], refs[-2], refs[-1]
    slots, width, _ = turned_ref.shape
    col = table_ref[slots, 0]
    sum_ref[...] = jnp.zeros_like(sum_ref)
    for s in range(slots):

        def put(blocks, s=s):
            near_ref[s] = blocks[0]

        second = table_ref[s, SECOND]

        def from_piece(p, s=s, second=second, put=put):
            pick(
                step,
                table_ref,
                s,
                lambda d: [old[p][d, second]],
                lambda j: [new[j][p][second]],
                put,
            )

        choose(table_ref[s, PIECE], 0, groups, from_piece)

    for s in range(slots):
        sum_ref[table_ref[s, FIRST]] += jnp.dot(
            near_ref[s], turned_ref[s], preferred_element_type=F32
        )

    for k in range(cols):
        start = pl.multiple_of((col ^ k) * width, width)
        outs[k][...] = sum_ref[:, :, pl.ds(start, width)].astype(outs[k].dtype)


def shards(pair_list, near_tile_block, history, excitation, diagonal):
    groups = lax.axis_size("pairs")
    cols = lax.axis_size("cols")
    planes = groups // CORES
    delays, clusters, excite, width = history.shape
    slots = pair_list.shape[0]
    block = (clusters, excite, width)

    smem = pl.BlockSpec(memory_space=pltpu.SMEM)
    vmem = pl.BlockSpec(memory_space=pltpu.VMEM)
    anywhere = pl.BlockSpec(memory_space=pl.ANY)
    rows = near_tile_block.shape[1]
    cost = pl.CostEstimate(
        flops=2 * near_tile_block.size * excite,
        bytes_accessed=2 * near_tile_block.size,
        transcendentals=0,
    )
    limit = pltpu.CompilerParams(vmem_limit_bytes=16 * 2**20)
    table = pl.pallas_call(
        table_kernel,
        out_shape=pltpu.SMEM((slots + 1, 5), jnp.int32),
        in_specs=[smem],
        out_specs=smem,
        compiler_params=pltpu.CompilerParams(vmem_limit_bytes=2**20),
        name="table",
    )(pair_list)
    def spread_cols(x):
        got = {0: x}
        for k in far_first(cols):
            got[k] = lax.ppermute(x, "cols", swapped(cols, k))
        return [got[k] for k in range(cols)]

    def spread_planes(x):
        got = {0: x}
        for k in far_first(planes):
            got[k] = lax.ppermute(x, "pairs", swapped(groups, CORES * k))
        return [got[k] for k in range(planes)]

    def spread_cores(xs):
        return [y for x in xs for y in (x, lax.ppermute(x, "pairs", swapped(groups, 1)))]

    def backward(step, old, new):
        return pl.pallas_call(
            functools.partial(backward_kernel, step, groups, cols),
            out_shape=(
                jax.ShapeDtypeStruct((planes, *block), F32),
                jax.ShapeDtypeStruct((planes, *block), BF16),
            ),
            in_specs=[smem]
            + [vmem] * (1 + cols * (1 + step)),
            out_specs=(vmem, vmem),
            scratch_shapes=[
                pltpu.VMEM((slots, excite, rows), BF16),
                pltpu.VMEM((groups, *block), F32),
            ],
            cost_estimate=cost,
            compiler_params=limit,
            name=f"backward{step}",
        )(table, near_tile_block, *old, *[x for n in new for x in n])

    def forward(step, old, new, after):
        return pl.pallas_call(
            functools.partial(forward_kernel, step, groups, cols),
            out_shape=[jax.ShapeDtypeStruct(block, F32)]
            + [jax.ShapeDtypeStruct(block, BF16)] * (cols - 1),
            in_specs=[smem]
            + [vmem] * (1 + groups + (planes + 1) * step)
            + [anywhere] * len(after),
            out_specs=[vmem] * cols,
            scratch_shapes=[
                pltpu.VMEM((slots, excite, width), BF16),
                pltpu.VMEM((clusters, excite, rows), F32),
            ],
            cost_estimate=cost,
            compiler_params=limit,
            name=f"forward{step}",
        )(table, turned, *old, *[x for n in new for x in n], *after)

    rounded = history.astype(BF16)
    planes_next = spread_planes(rounded)
    cols_next = spread_cols(rounded)
    cols_next[-1], tile = lax.optimization_barrier((cols_next[-1], near_tile_block))
    turned = pl.pallas_call(
        turn_kernel,
        out_shape=pltpu.VMEM((slots, width, rows), BF16),
        in_specs=[vmem],
        out_specs=vmem,
        cost_estimate=cost,
        compiler_params=limit,
        name="turn",
    )(tile)
    rows_of, near_of, results = [], [], []
    for step in range(STEPS):
        if step == 0:
            cols_next, planes_next[-2], turned, table = lax.optimization_barrier((cols_next, planes_next[-2], turned, table))
        rows_of.append(cols_next)
        same, other = backward(step, rows_of[0], rows_of[1:])
        if step:
            planes_next, same, other = lax.optimization_barrier((planes_next, same, other))
        mate = lax.ppermute(other, "pairs", swapped(groups, 1))
        if step == 0:
            near_of.append(spread_cores(planes_next))
        else:
            mates = lax.ppermute(jnp.stack(planes_next), "pairs", swapped(groups, 1))
            near_of.append([*planes_next, mates])
        sent = [same[k] + mate[k].astype(F32) for k in range(planes)]
        sent[1:] = [x.astype(BF16) for x in sent[1:]]
        field = sent[0]
        for k in far_first(planes):
            field += lax.ppermute(sent[k], "pairs", swapped(groups, CORES * k)).astype(F32)
        parts = forward(step, near_of[0], near_of[1:], sent)
        field += parts[0]
        for k in far_first(cols):
            field += lax.ppermute(parts[k], "cols", swapped(cols, k)).astype(F32)
        fresh = (excitation[step] - field) / diagonal[:, None, :]
        results.append(fresh)
        if step + 1 < STEPS:
            newest = fresh.astype(BF16)
            planes_next = spread_planes(newest)
            cols_next = spread_cols(newest)
    return jnp.stack(results)


def solution(mesh):
    placed = (
        P("pairs", None),
        P("pairs", None, "cols"),
        P(None, "pairs", None, "cols"),
        P(None, "pairs", None, "cols"),
        P("pairs", "cols"),
    )
    return jax.shard_map(
        shards,
        mesh=mesh,
        in_specs=placed,
        out_specs=P(None, "pairs", None, "cols"),
        check_vma=False,
    )
```
